32 devices in a mesh: ckpt: 8 (over y, x, core), lat: 4 (over z).
Axes of the slice: x: 2, y: 2, z: 4, core: 2. Of those that a mesh axis runs over, the one named last changes fastest.
Arguments:
- hidden_in: bfloat16 [16, 512, 1024], P('ckpt', None, 'lat'), may hold values from -6 to 6
- ln_gain: float32 [16, 1024], P('ckpt'), may hold values from 0.4 to 1.6
- ln_bias: float32 [16, 1024], P('ckpt'), may hold values from -2.5 to 2.5
- w_in: bfloat16 [16, 1024, 4096], P('ckpt', None, 'lat'), may hold values from -0.1875 to 0.1875
- b_in: float32 [16, 4096], P('ckpt', 'lat'), may hold values from -3 to 3
- w_out: bfloat16 [16, 4096, 1024], P('ckpt', 'lat'), may hold values from -0.09375 to 0.09375
- b_out: float32 [16, 1024], P('ckpt'), may hold values from -3 to 3
- w_enc: bfloat16 [16, 1024, 8192], P('ckpt', None, 'lat'), may hold values from -0.046875 to 0.046875
- b_enc: float32 [8192], P('lat'), may hold values from -3 to 3
- w_dec: bfloat16 [16, 8192, 1024], P('ckpt', 'lat'), may hold values from -6 to 6
- b_dec: float32 [16, 1024], P('ckpt'), may hold values from -3 to 3
Outputs:
- grad_enc: bfloat16 [16, 1024, 8192], P('ckpt', None, 'lat')
- grad_benc: float32 [8192], P('lat')
- grad_dec: bfloat16 [16, 8192, 1024], P('ckpt', 'lat')
The draws below stay inside these ranges and needn't reach their ends.
All inputs are finite; a program needn't handle non-finite values.
Results may differ from the reference program's by a relative error of at most 0.0075.
Values may be sent and summed in bfloat16 or wider, within the bound.
A program may use at most 128 MiB of HBM per device.

```python
import math
import jax
import jax.numpy as jnp
from jax import lax

D = 1024
FF = 4096
LATENTS = 8192
TOK = 512
CKPTS = 16


def draw_w_dec(key, part):
    base = jax.random.normal(jax.random.fold_in(key, 11), (CKPTS, LATENTS, D), jnp.float32)
    base = jnp.clip(base, -6.0, 6.0) / jnp.sqrt(jnp.float32(LATENTS))
    place = jnp.arange(CKPTS).astype(jnp.float32) / jnp.float32(max(CKPTS - 1, 1)) - 0.5
    ramp = jnp.exp(jnp.log(6.0) * place)
    return jnp.clip(base * ramp[:, None, None], -6.0, 6.0).astype(jnp.bfloat16)


def block_scale(stream_key, dims, shards, least, top_value):
    def one(dim, shards_of):
        draws = jax.random.uniform(jax.random.fold_in(jax.random.fold_in(stream_key, 6), dim), (shards_of,), jnp.float32, least / len(shards), top_value / len(shards))
        return jnp.repeat(jnp.exp(draws), dims[dim] // shards_of).reshape((-1,) + (1,) * (len(dims) - dim - 1))

    loudness = one(*shards[0])
    for cut in shards[1:]:
        loudness = loudness * one(*cut)
    return loudness


def centred(own_key, extent, scale, limit, cuts=(), kind=jnp.bfloat16):
    drawn = scale * jax.random.normal(own_key, extent, jnp.float32)
    if cuts:
        drawn = drawn * block_scale(own_key, extent, cuts, -0.22, 0.18)
    return jnp.clip(drawn, -limit, limit).astype(kind)


def setup_inputs(seed: int = 0) -> dict:
    keys = jax.random.split(jax.random.key(seed), 12)
    return {
        "hidden_in": centred(keys[0], (CKPTS, TOK, D), 1.0, 6.0, ((0, 8), (2, 4))),
        "ln_gain": jnp.clip(1.0 + 0.12 * jax.random.normal(keys[1], (CKPTS, D), jnp.float32), 0.4, 1.6),
        "ln_bias": centred(keys[2], (CKPTS, D), 0.4, 2.5, ((0, 8),), jnp.float32),
        "w_in": centred(keys[3], (CKPTS, D, FF), D ** -0.5, 0.1875, ((0, 8), (2, 4))),
        "b_in": centred(keys[4], (CKPTS, FF), 0.5, 3.0, ((0, 8), (1, 4)), jnp.float32),
        "w_out": centred(keys[5], (CKPTS, FF, D), FF ** -0.5, 0.09375, ((0, 8), (1, 4))),
        "b_out": centred(keys[6], (CKPTS, D), 0.5, 3.0, ((0, 8),), jnp.float32),
        "w_enc": centred(keys[7], (CKPTS, D, LATENTS), (CKPTS * D) ** -0.5, 0.046875, ((0, 8), (2, 4))),
        "b_enc": centred(keys[8], (LATENTS,), 0.5, 3.0, ((0, 4),), jnp.float32),
        "w_dec": draw_w_dec(jax.random.fold_in(keys[11], 71), 0),
        "b_dec": centred(keys[10], (CKPTS, D), 0.5, 3.0, ((0, 8),), jnp.float32),
    }


norm_eps = 1e-05
row_eps = 1e-06
sparsity_weight = 0.2

def section_one(parts):
    hidden, gain, bias, w_first, b_first, w_second, b_second = parts
    floats = hidden.astype(jnp.float32)
    center = floats - lax.optimization_barrier(jnp.mean(floats, -1, keepdims=True))
    spread = lax.optimization_barrier(jnp.mean(center * center, -1, keepdims=True))
    normed = (center * lax.rsqrt(spread + norm_eps) * gain + bias).astype(jnp.bfloat16)
    raised = jnp.dot(normed, w_first, preferred_element_type=jnp.float32) + b_first
    active = jax.nn.gelu(raised, approximate=False).astype(jnp.bfloat16)
    return (floats + jnp.dot(active, w_second, preferred_element_type=jnp.float32) + b_second).astype(jnp.bfloat16)

def reference(hidden_in, ln_gain, ln_bias, w_in, b_in, w_out, b_out, w_enc, b_enc, w_dec, b_dec):
    scale = 1.0 / math.sqrt(TOK)
    acts = lax.map(section_one, (hidden_in, ln_gain, ln_bias, w_in, b_in, w_out, b_out))

    def add_encoded(carry, pair):
        return (carry + jnp.dot(pair[0], pair[1], preferred_element_type=jnp.float32), None)
    pre = lax.scan(add_encoded, jnp.zeros((TOK, LATENTS), jnp.float32), (acts, w_enc))[0] + b_enc
    feat = jnp.maximum(pre, 0.0).astype(jnp.bfloat16)

    def row_norms(weight):
        wide = weight.astype(jnp.float32)
        return jnp.sqrt(lax.optimization_barrier(jnp.sum(wide * wide, -1)) + row_eps)
    norms = lax.map(row_norms, w_dec)
    total = lax.optimization_barrier(jnp.sum(norms, 0))

    def residual(parts):
        act, weight, bias = parts
        resid = jnp.dot(feat, weight, preferred_element_type=jnp.float32) + bias - act.astype(jnp.float32)
        return (resid * scale).astype(jnp.bfloat16)
    dres = lax.map(residual, (acts, w_dec, b_dec))

    def add_back(carry, pair):
        return (carry + jnp.dot(pair[0], pair[1].T, preferred_element_type=jnp.float32), None)
    dfeat = lax.scan(add_back, jnp.zeros((TOK, LATENTS), jnp.float32), (dres, w_dec))[0]
    dfeat = dfeat + sparsity_weight * scale * total
    dpre = jnp.where(pre > 0.0, dfeat, 0.0).astype(jnp.bfloat16)

    def encoder_grad(act):
        return jnp.dot(act.T, dpre, preferred_element_type=jnp.float32).astype(jnp.bfloat16)
    grad_enc = lax.map(encoder_grad, acts)
    grad_benc = lax.optimization_barrier(jnp.sum(dpre.astype(jnp.float32), 0))
    column = lax.optimization_barrier(jnp.sum(feat.astype(jnp.float32), 0))

    def decoder_grad(parts):
        grads, weight, norm_row = parts
        main = jnp.dot(feat.T, grads, preferred_element_type=jnp.float32)
        extra = sparsity_weight * scale * column[:, None] * weight.astype(jnp.float32) / norm_row[:, None]
        return (main + extra).astype(jnp.bfloat16)
    grad_dec = lax.map(decoder_grad, (dres, w_dec, norms))
    return (grad_enc, grad_benc, grad_dec)
```

```python
import functools
import math

import jax
import jax.numpy as jnp
from jax import lax
from jax.experimental import pallas as pl
from jax.experimental.pallas import tpu as pltpu
from jax.sharding import PartitionSpec as P

norm_eps = 1e-05
row_eps = 1e-06
sparsity_weight = 0.2
MESH = pl.DeviceIdType.MESH
BF = jnp.bfloat16
F32 = jnp.float32


def kernel(
    nl, nc, chunks, order,
    hid, gain, bias, w_in, b_in, w_out, b_out, w_enc, b_enc, w_dec, b_dec, total,
    acts, dres, feat, dpre,
    full, vin, vout, venc, vdec, normed, active, part, part2, zbuf, ppart, dpart, cbuf, pre,
    wsem, own_sem, zsend, zrecv, csend, crecv,
):
    K, tok, cols = hid.shape
    D = cols * nl
    T = tok // chunks
    zr = T // nl
    cr = T // nc
    ff = vin.shape[2]
    lat = venc.shape[2]
    scale = 1.0 / math.sqrt(tok)
    lz = lax.axis_index("lat")
    lc = lax.axis_index("ckpt")

    barrier = pltpu.get_barrier_semaphore()
    for off in range(1, nl):
        pl.semaphore_signal(
            barrier, inc=1, device_id={"lat": lax.rem(lz + off, nl)}, device_id_type=MESH
        )
    for off in range(1, nc):
        pl.semaphore_signal(
            barrier, inc=1, device_id={"ckpt": lax.rem(lc + off, nc)}, device_id_type=MESH
        )
    pl.semaphore_wait(barrier, nl + nc - 2)

    def zcopy(stage, c, off, src, dst):
        return pltpu.make_async_remote_copy(
            src_ref=src, dst_ref=dst,
            send_sem=zsend.at[stage, c, off - 1], recv_sem=zrecv.at[stage, c, off - 1],
            device_id={"lat": lax.rem(lz + off, nl)}, device_id_type=MESH,
        )

    def ccopy(stage, c, off, src, dst):
        return pltpu.make_async_remote_copy(
            src_ref=src, dst_ref=dst,
            send_sem=csend.at[stage, c, off - 1], recv_sem=crecv.at[stage, c, off - 1],
            device_id={"ckpt": lax.rem(lc + off, nc)}, device_id_type=MESH,
        )

    def rows(c):
        return pl.ds(c * T, T)

    def zrows(c, i):
        return pl.ds(pl.multiple_of(c * T + i * zr, zr), zr)

    def crows(c, i):
        return pl.ds(pl.multiple_of(c * T + i * cr, cr), cr)

    def hid_copy(c, off):
        mine = pl.ds(pl.multiple_of(lz * cols, cols), cols)
        return zcopy(0, c, off, hid.at[:, rows(c), :], full.at[:, rows(c), mine])

    def zscatter(stage, slot, source):
        def make(c, off):
            dest = lax.rem(lz + off, nl)
            return zcopy(stage, c, off, source.at[:, zrows(c, dest), :], zbuf.at[slot, c, off - 1])
        return make

    def zgather(stage, ref):
        def make(c, off):
            piece = ref.at[:, zrows(c, lz), :]
            return zcopy(stage, c, off, piece, piece)
        return make

    def cscatter(stage, slot, source):
        def make(c, off):
            dest = lax.rem(lc + off, nc)
            return ccopy(stage, c, off, source.at[crows(c, dest), :], cbuf.at[slot, c, off - 1])
        return make

    def cgather(stage, ref):
        def make(c, off):
            piece = ref.at[crows(c, lc), :]
            return ccopy(stage, c, off, piece, piece)
        return make

    moves = {
        0: (hid_copy, nl),
        1: (zscatter(1, 0, part), nl),
        2: (zgather(2, acts), nl),
        3: (cscatter(0, 0, ppart), nc),
        4: (cgather(1, feat), nc),
        5: (zscatter(3, 1, part2), nl),
        6: (zgather(4, dres), nl),
        7: (cscatter(2, 1, dpart), nc),
        8: (cgather(3, dpre), nc),
    }

    def send(stage, c):
        make, n = moves[stage]
        for off in range(1, n):
            make(c, off).start()

    def recv(stage, c):
        make, n = moves[stage]
        for off in range(1, n):
            make(c, off).wait_recv()

    own = pltpu.make_async_copy(
        hid, full.at[:, :, pl.ds(pl.multiple_of(lz * cols, cols), cols)], own_sem
    )
    loads = [
        pltpu.make_async_copy(src, dst, wsem.at[i])
        for i, (src, dst) in enumerate(
            ((w_in, vin), (w_out, vout), (w_enc, venc), (w_dec, vdec))
        )
    ]
    for c in range(chunks):
        send(0, c)
    own.start()
    for load in loads:
        load.start()

    ft = min(256, ff)
    dt = min(256, D)
    lt = min(256, lat)

    def tile(i, t):
        return pl.ds(pl.multiple_of(i * t, t), t)

    def mlp(c):
        if c == 0:
            own.wait()
        recv(0, c)
        if c == 0:
            loads[0].wait()
            loads[1].wait()
        for k in range(K):
            floats = full[k, rows(c), :].astype(F32)
            center = floats - jnp.mean(floats, -1, keepdims=True)
            spread = jnp.mean(center * center, -1, keepdims=True)
            normed[...] = (
                center * lax.rsqrt(spread + norm_eps) * gain[k : k + 1, :] + bias[k : k + 1, :]
            ).astype(BF)

            @pl.loop(0, ff // ft)
            def _(i):
                s = tile(i, ft)
                h = jnp.dot(normed[...], vin[k, :, s], preferred_element_type=F32)
                h = h + b_in[k : k + 1, s]
                active[:, s] = (0.5 * h * (1.0 + lax.erf(h * math.sqrt(0.5)))).astype(BF)

            @pl.loop(0, D // dt)
            def _(i):
                s = tile(i, dt)
                part[k, rows(c), s] = jnp.dot(
                    active[...], vout[k, :, s], preferred_element_type=F32
                ).astype(BF)
        send(1, c)

    def make_acts(c):
        recv(1, c)
        for k in range(K):
            mine = zrows(c, lz)
            value = part[k, mine, :].astype(F32)
            for off in range(1, nl):
                value = value + zbuf[0, c, off - 1, k].astype(F32)
            value = value + full[k, mine, :].astype(F32) + b_out[k : k + 1, :]
            acts[k, mine, :] = value.astype(BF)
        send(2, c)

    def encode(c):
        recv(2, c)
        if c == 0:
            loads[2].wait()

        @pl.loop(0, lat // lt)
        def _(i):
            s = tile(i, lt)
            value = jnp.dot(acts[0, rows(c), :], venc[0, :, s], preferred_element_type=F32)
            for k in range(1, K):
                value = value + jnp.dot(
                    acts[k, rows(c), :], venc[k, :, s], preferred_element_type=F32
                )
            ppart[rows(c), s] = value.astype(ppart.dtype)
        send(3, c)

    def make_feat(c):
        recv(3, c)
        value = ppart[crows(c, lc), :].astype(F32)
        for off in range(1, nc):
            value = value + cbuf[0, c, off - 1].astype(F32)
        value = value + b_enc[...]
        pre[c] = value
        feat[crows(c, lc), :] = jnp.maximum(value, 0.0).astype(BF)
        send(4, c)

    def decode(c):
        recv(4, c)
        if c == 0:
            loads[3].wait()
        for k in range(K):

            @pl.loop(0, D // dt)
            def _(i):
                s = tile(i, dt)
                part2[k, rows(c), s] = jnp.dot(
                    feat[rows(c), :], vdec[k, :, s], preferred_element_type=F32
                ).astype(BF)
        send(5, c)

    def make_dres(c):
        recv(5, c)
        for k in range(K):
            mine = zrows(c, lz)
            value = part2[k, mine, :].astype(F32)
            for off in range(1, nl):
                value = value + zbuf[1, c, off - 1, k].astype(F32)
            value = value + b_dec[k : k + 1, :] - acts[k, mine, :].astype(F32)
            dres[k, mine, :] = (value * scale).astype(BF)
        send(6, c)

    def back(c):
        recv(6, c)
        dims = (((1,), (1,)), ((), ()))

        @pl.loop(0, lat // lt)
        def _(i):
            s = tile(i, lt)
            value = sparsity_weight * scale * total[:, s]
            for k in range(K):
                value = value + lax.dot_general(
                    dres[k, rows(c), :], vdec[k, s, :], dims, preferred_element_type=F32
                )
            dpart[rows(c), s] = value.astype(BF)
        send(7, c)

    def make_dpre(c):
        recv(7, c)
        value = dpart[crows(c, lc), :].astype(F32)
        for off in range(1, nc):
            value = value + cbuf[1, c, off - 1].astype(F32)
        dpre[crows(c, lc), :] = jnp.where(pre[c] > 0.0, value, 0.0).astype(BF)
        send(8, c)

    def last(c):
        recv(8, c)

    steps = (mlp, make_acts, encode, make_feat, decode, make_dres, back, make_dpre, last)
    for step, c in order:
        steps[step](c)
    for stage, (make, n) in moves.items():
        for c in range(chunks):
            for off in range(1, n):
                make(c, off).wait_send()


def fused(hidden_in, ln_gain, ln_bias, w_in, b_in, w_out, b_out, w_enc, b_enc, w_dec, b_dec, total,
          nl, nc, chunks, skew):
    K, tok, cols = hidden_in.shape
    D = cols * nl
    ff = w_in.shape[2]
    lat = w_enc.shape[2]
    T = tok // chunks
    steps = 9
    order = sorted(
        ((s, c) for s in range(steps) for c in range(chunks)), key=lambda p: (p[0] + skew * p[1], p[1])
    )
    VM = pl.BlockSpec(memory_space=pltpu.VMEM)
    HB = pl.BlockSpec(memory_space=pl.ANY)
    flops = 2 * tok * K * (2 * D * ff + 3 * D * lat)
    return pl.pallas_call(
        functools.partial(kernel, nl, nc, chunks, order),
        out_shape=(
            jax.ShapeDtypeStruct((K, tok, D), BF),
            jax.ShapeDtypeStruct((K, tok, D), BF),
            jax.ShapeDtypeStruct((tok, lat), BF),
            jax.ShapeDtypeStruct((tok, lat), BF),
        ),
        in_specs=[HB, VM, VM, HB, VM, HB, VM, HB, VM, HB, VM, VM],
        out_specs=(VM, VM, VM, VM),
        scratch_shapes=[
            pltpu.VMEM((K, tok, D), BF),
            pltpu.VMEM(w_in.shape, BF),
            pltpu.VMEM(w_out.shape, BF),
            pltpu.VMEM(w_enc.shape, BF),
            pltpu.VMEM(w_dec.shape, BF),
            pltpu.VMEM((T, D), BF),
            pltpu.VMEM((T, ff), BF),
            pltpu.VMEM((K, tok, D), BF),
            pltpu.VMEM((K, tok, D), BF),
            pltpu.VMEM((2, chunks, nl - 1, K, T // nl, D), BF),
            pltpu.VMEM((tok, lat), BF),
            pltpu.VMEM((tok, lat), BF),
            pltpu.VMEM((2, chunks, nc - 1, T // nc, lat), BF),
            pltpu.VMEM((chunks, T // nc, lat), F32),
            pltpu.SemaphoreType.DMA((4,)),
            pltpu.SemaphoreType.DMA,
            pltpu.SemaphoreType.DMA((5, chunks, nl - 1)),
            pltpu.SemaphoreType.DMA((5, chunks, nl - 1)),
            pltpu.SemaphoreType.DMA((4, chunks, nc - 1)),
            pltpu.SemaphoreType.DMA((4, chunks, nc - 1)),
        ],
        compiler_params=pltpu.CompilerParams(
            collective_id=0, has_side_effects=True, vmem_limit_bytes=62 * 1024 * 1024
        ),
        cost_estimate=pl.CostEstimate(flops=flops, bytes_accessed=40 << 20, transcendentals=tok * ff),
    )(hidden_in, ln_gain, ln_bias, w_in, b_in, w_out, b_out, w_enc, b_enc[None, :], w_dec, b_dec,
      total[None, :])


def plain(hidden_in, ln_gain, ln_bias, w_in, b_in, w_out, b_out, w_enc, b_enc, w_dec, b_dec, total):
    tokens = hidden_in.shape[1]
    feat_cols = hidden_in.shape[2]
    scale = 1.0 / math.sqrt(tokens)
    lat_index = lax.axis_index("lat")
    whole = lax.all_gather(hidden_in, "lat", axis=2, tiled=True)
    floats = whole.astype(F32)
    center = floats - jnp.mean(floats, -1, keepdims=True)
    spread = jnp.mean(center * center, -1, keepdims=True)
    normed = (
        center * lax.rsqrt(spread + norm_eps) * ln_gain[:, None, :] + ln_bias[:, None, :]
    ).astype(BF)
    raised = jnp.einsum("ctd,cdf->ctf", normed, w_in, preferred_element_type=F32) + b_in[:, None, :]
    active = jax.nn.gelu(raised, approximate=False).astype(BF)
    terms = jnp.einsum("ctf,cfd->ctd", active, w_out, preferred_element_type=F32)
    share = lax.psum_scatter(terms, "lat", scatter_dimension=2, tiled=True)
    out_bias = lax.dynamic_slice_in_dim(b_out, lat_index * feat_cols, feat_cols, 1)
    piece = (hidden_in.astype(F32) + share + out_bias[:, None, :]).astype(BF)
    acts = lax.all_gather(piece, "lat", axis=2, tiled=True)
    pre_sum, total = lax.psum(
        (jnp.einsum("ctd,cdl->tl", acts, w_enc, preferred_element_type=F32), total), "ckpt"
    )
    pre = pre_sum + b_enc[None, :]
    feat = jnp.maximum(pre, 0.0).astype(BF)
    recon_terms = jnp.einsum("tl,cld->ctd", feat, w_dec, preferred_element_type=F32)
    recon = lax.psum(recon_terms.astype(BF), "lat").astype(F32)
    dres = ((recon + b_dec[:, None, :] - acts.astype(F32)) * scale).astype(BF)
    dfeat = lax.psum(
        jnp.einsum("ctd,cld->tl", dres, w_dec, preferred_element_type=F32).astype(BF), "ckpt"
    ).astype(F32) + (sparsity_weight * scale * total)[None, :]
    dpre = jnp.where(pre > 0.0, dfeat, 0.0).astype(BF)
    return acts, dres, feat, dpre


def on_device(nl, nc, hidden_in, ln_gain, ln_bias, w_in, b_in, w_out, b_out, w_enc, b_enc, w_dec, b_dec):
    K, tok, cols = hidden_in.shape
    scale = 1.0 / math.sqrt(tok)
    chunks = 2
    T = tok // chunks
    wide_dec = w_dec.astype(F32)
    norms = jnp.sqrt(jnp.sum(wide_dec * wide_dec, 2) + row_eps)
    local_total = jnp.sum(norms, 0)
    args = (hidden_in, ln_gain, ln_bias, w_in, b_in, w_out, b_out, w_enc, b_enc, w_dec, b_dec,
            local_total)
    if cols % 128 == 0 and T % (16 * nl) == 0 and T % (16 * nc) == 0:
        acts, dres, feat, dpre = fused(*args, nl, nc, chunks, 2)
    else:
        acts, dres, feat, dpre = plain(*args)
    grad_enc = jnp.einsum("ctd,tl->cdl", acts, dpre, preferred_element_type=F32).astype(BF)
    grad_benc = jnp.sum(dpre.astype(F32), 0)
    column = jnp.sum(feat.astype(F32), 0)
    main = jnp.einsum("tl,ctd->cld", feat, dres, preferred_element_type=F32)
    extra = sparsity_weight * scale * column[None, :, None] * wide_dec / norms[:, :, None]
    grad_dec = (main + extra).astype(BF)
    return (grad_enc, grad_benc, grad_dec)


def solution(mesh):
    placed = (
        P("ckpt", None, "lat"),
        P("ckpt", None),
        P("ckpt", None),
        P("ckpt", None, "lat"),
        P("ckpt", "lat"),
        P("ckpt", "lat", None),
        P("ckpt", None),
        P("ckpt", None, "lat"),
        P("lat"),
        P("ckpt", "lat", None),
        P("ckpt", None),
    )
    return jax.shard_map(
        functools.partial(on_device, mesh.shape["lat"], mesh.shape["ckpt"]),
        mesh=mesh,
        in_specs=placed,
        out_specs=(P("ckpt", None, "lat"), P("lat"), P("ckpt", "lat", None)),
        check_vma=False,
    )
```

```python
import functools
import math

import jax
import jax.numpy as jnp
from jax import lax
from jax.experimental import pallas as pl
from jax.experimental.pallas import tpu as pltpu
from jax.sharding import PartitionSpec as P

norm_eps = 1e-05
row_eps = 1e-06
sparsity_weight = 0.2
MESH = pl.DeviceIdType.MESH
BF = jnp.bfloat16
F32 = jnp.float32


def kernel(
    nl, nc, chunks, order,
    hid, gain, bias, w_in, b_in, w_out, b_out, w_enc, b_enc, w_dec, b_dec,
    acts, dres, feat, dpre,
    full, vin, vout, venc, vdec, normed, active, part, part2, zbuf, ppart, dpart, cbuf, pre, total,
    wsem, own_sem, zsend, zrecv, csend, crecv,
):
    K, tok, cols = hid.shape
    D = cols * nl
    T = tok // chunks
    zr = T // nl
    cr = T // nc
    ff = vin.shape[2]
    lat = venc.shape[2]
    scale = 1.0 / math.sqrt(tok)
    lz = lax.axis_index("lat")
    lc = lax.axis_index("ckpt")

    barrier = pltpu.get_barrier_semaphore()
    for off in range(1, nl):
        pl.semaphore_signal(
            barrier, inc=1, device_id={"lat": lax.rem(lz + off, nl)}, device_id_type=MESH
        )
    for off in range(1, nc):
        pl.semaphore_signal(
            barrier, inc=1, device_id={"ckpt": lax.rem(lc + off, nc)}, device_id_type=MESH
        )
    pl.semaphore_wait(barrier, nl + nc - 2)

    def zcopy(stage, c, k, off, src, dst):
        return pltpu.make_async_remote_copy(
            src_ref=src, dst_ref=dst,
            send_sem=zsend.at[stage, c, k, off - 1], recv_sem=zrecv.at[stage, c, k, off - 1],
            device_id={"lat": lax.rem(lz + off, nl)}, device_id_type=MESH,
        )

    def ccopy(stage, c, off, src, dst):
        return pltpu.make_async_remote_copy(
            src_ref=src, dst_ref=dst,
            send_sem=csend.at[stage, c, off - 1], recv_sem=crecv.at[stage, c, off - 1],
            device_id={"ckpt": lax.rem(lc + off, nc)}, device_id_type=MESH,
        )

    def rows(c):
        return pl.ds(c * T, T)

    def zrows(c, i):
        return pl.ds(pl.multiple_of(c * T + i * zr, zr), zr)

    def crows(c, i):
        return pl.ds(pl.multiple_of(c * T + i * cr, cr), cr)

    def hid_copy(c, k, off):
        mine = pl.ds(pl.multiple_of(lz * cols, cols), cols)
        return zcopy(0, c, k, off, hid.at[k, rows(c), :], full.at[k, rows(c), mine])

    def zscatter(stage, slot, source):
        def make(c, k, off):
            dest = lax.rem(lz + off, nl)
            return zcopy(
                stage, c, k, off, source.at[k, zrows(c, dest), :], zbuf.at[slot, c, off - 1, k]
            )
        return make

    def zgather(stage, ref):
        def make(c, k, off):
            piece = ref.at[k, zrows(c, lz), :]
            return zcopy(stage, c, k, off, piece, piece)
        return make

    def cscatter(stage, slot, source):
        def make(c, k, off):
            dest = lax.rem(lc + off, nc)
            return ccopy(stage, c, off, source.at[crows(c, dest), :], cbuf.at[slot, c, off - 1])
        return make

    def cgather(stage, ref):
        def make(c, k, off):
            piece = ref.at[crows(c, lc), :]
            return ccopy(stage, c, off, piece, piece)
        return make

    moves = {
        0: (hid_copy, nl),
        1: (zscatter(1, 0, part), nl),
        2: (zgather(2, acts), nl),
        3: (cscatter(0, 0, ppart), nc),
        4: (cgather(1, feat), nc),
        5: (zscatter(3, 1, part2), nl),
        6: (zgather(4, dres), nl),
        7: (cscatter(2, 1, dpart), nc),
        8: (cgather(3, dpre), nc),
    }

    parts = {stage: K if stage in (0, 1, 2, 5, 6) else 1 for stage in moves}

    def send(stage, c, k=0):
        make, n = moves[stage]
        for off in range(1, n):
            make(c, k, off).start()

    def recv(stage, c, k=0):
        make, n = moves[stage]
        for off in range(1, n):
            make(c, k, off).wait_recv()

    own = pltpu.make_async_copy(
        hid, full.at[:, :, pl.ds(pl.multiple_of(lz * cols, cols), cols)], own_sem
    )
    loads = [
        pltpu.make_async_copy(src, dst, wsem.at[i])
        for i, (src, dst) in enumerate(
            ((w_in, vin), (w_out, vout), (w_enc, venc), (w_dec, vdec))
        )
    ]
    for c in range(chunks):
        for k in range(K):
            send(0, c, k)
    own.start()
    for load in loads:
        load.start()

    ft = min(256, ff)
    dt = min(256, D)
    lt = min(256, lat)

    def tile(i, t):
        return pl.ds(pl.multiple_of(i * t, t), t)

    def add_norms():
        @pl.loop(0, lat // lt)
        def _(i):
            s = tile(i, lt)
            value = jnp.zeros((lt, 1), F32)
            for k in range(K):
                w = vdec[k, s, :].astype(F32)
                value = value + jnp.sqrt(jnp.sum(w * w, -1, keepdims=True) + row_eps)
            total[:, s] = jnp.broadcast_to(value, (lt, 128)).T[0:8, :]

    def mlp(c):
        if c == 0:
            own.wait()
            for load in loads:
                load.wait()
            add_norms()
        for k in range(K):
            recv(0, c, k)
            floats = full[k, rows(c), :].astype(F32)
            center = floats - jnp.mean(floats, -1, keepdims=True)
            spread = jnp.mean(center * center, -1, keepdims=True)
            normed[...] = (
                center * lax.rsqrt(spread + norm_eps) * gain[k : k + 1, :] + bias[k : k + 1, :]
            ).astype(BF)

            @pl.loop(0, ff // ft)
            def _(i):
                s = tile(i, ft)
                h = jnp.dot(normed[...], vin[k, :, s], preferred_element_type=F32)
                h = h + b_in[k : k + 1, s]
                active[:, s] = (0.5 * h * (1.0 + lax.erf(h * math.sqrt(0.5)))).astype(BF)

            @pl.loop(0, D // dt)
            def _(i):
                s = tile(i, dt)
                part[k, rows(c), s] = jnp.dot(
                    active[...], vout[k, :, s], preferred_element_type=F32
                ).astype(BF)

            send(1, c, k)

    def make_acts(c):
        for k in range(K):
            recv(1, c, k)
            mine = zrows(c, lz)
            value = part[k, mine, :].astype(F32)
            for off in range(1, nl):
                value = value + zbuf[0, c, off - 1, k].astype(F32)
            value = value + full[k, mine, :].astype(F32) + b_out[k : k + 1, :]
            acts[k, mine, :] = value.astype(BF)
            send(2, c, k)

    def encode(c):
        for k in range(K):
            recv(2, c, k)

        @pl.loop(0, lat // lt)
        def _(i):
            s = tile(i, lt)
            value = jnp.dot(acts[0, rows(c), :], venc[0, :, s], preferred_element_type=F32)
            for k in range(1, K):
                value = value + jnp.dot(
                    acts[k, rows(c), :], venc[k, :, s], preferred_element_type=F32
                )
            ppart[rows(c), s] = value.astype(ppart.dtype)
        send(3, c)

    def make_feat(c):
        recv(3, c)
        value = ppart[crows(c, lc), :].astype(F32)
        for off in range(1, nc):
            value = value + cbuf[0, c, off - 1].astype(F32)
        value = value + b_enc[...]
        pre[c] = value
        feat[crows(c, lc), :] = jnp.maximum(value, 0.0).astype(BF)
        send(4, c)

    def decode(c):
        recv(4, c)
        for k in range(K):

            @pl.loop(0, D // dt)
            def _(i):
                s = tile(i, dt)
                part2[k, rows(c), s] = jnp.dot(
                    feat[rows(c), :], vdec[k, :, s], preferred_element_type=F32
                ).astype(BF)

            send(5, c, k)

    def make_dres(c):
        for k in range(K):
            recv(5, c, k)
            mine = zrows(c, lz)
            value = part2[k, mine, :].astype(F32)
            for off in range(1, nl):
                value = value + zbuf[1, c, off - 1, k].astype(F32)
            value = value + b_dec[k : k + 1, :] - acts[k, mine, :].astype(F32)
            dres[k, mine, :] = (value * scale).astype(BF)
            send(6, c, k)

    def back(c):
        for k in range(K):
            recv(6, c, k)
        dims = (((1,), (1,)), ((), ()))

        @pl.loop(0, lat // lt)
        def _(i):
            s = tile(i, lt)
            value = sparsity_weight * scale * total[0:1, s]
            for k in range(K):
                value = value + lax.dot_general(
                    dres[k, rows(c), :], vdec[k, s, :], dims, preferred_element_type=F32
                )
            dpart[rows(c), s] = value.astype(BF)
        send(7, c)

    def make_dpre(c):
        recv(7, c)
        value = dpart[crows(c, lc), :].astype(F32)
        for off in range(1, nc):
            value = value + cbuf[1, c, off - 1].astype(F32)
        dpre[crows(c, lc), :] = jnp.where(pre[c] > 0.0, value, 0.0).astype(BF)
        send(8, c)

    def last(c):
        recv(8, c)

    steps = (mlp, make_acts, encode, make_feat, decode, make_dres, back, make_dpre, last)
    for step, c in order:
        steps[step](c)
    for stage, (make, n) in moves.items():
        for c in range(chunks):
            for k in range(parts[stage]):
                for off in range(1, n):
                    make(c, k, off).wait_send()


def fused(hidden_in, ln_gain, ln_bias, w_in, b_in, w_out, b_out, w_enc, b_enc, w_dec, b_dec,
          nl, nc, chunks, skew):
    K, tok, cols = hidden_in.shape
    D = cols * nl
    ff = w_in.shape[2]
    lat = w_enc.shape[2]
    T = tok // chunks
    steps = 9
    order = sorted(
        ((s, c) for s in range(steps) for c in range(chunks)), key=lambda p: (p[0] + skew * p[1], p[1])
    )
    VM = pl.BlockSpec(memory_space=pltpu.VMEM)
    HB = pl.BlockSpec(memory_space=pl.ANY)
    flops = 2 * tok * K * (2 * D * ff + 3 * D * lat)
    return pl.pallas_call(
        functools.partial(kernel, nl, nc, chunks, order),
        out_shape=(
            jax.ShapeDtypeStruct((K, tok, D), BF),
            jax.ShapeDtypeStruct((K, tok, D), BF),
            jax.ShapeDtypeStruct((tok, lat), BF),
            jax.ShapeDtypeStruct((tok, lat), BF),
        ),
        in_specs=[HB, VM, VM, HB, VM, HB, VM, HB, VM, HB, VM],
        out_specs=(VM, VM, VM, VM),
        scratch_shapes=[
            pltpu.VMEM((K, tok, D), BF),
            pltpu.VMEM(w_in.shape, BF),
            pltpu.VMEM(w_out.shape, BF),
            pltpu.VMEM(w_enc.shape, BF),
            pltpu.VMEM(w_dec.shape, BF),
            pltpu.VMEM((T, D), BF),
            pltpu.VMEM((T, ff), BF),
            pltpu.VMEM((K, tok, D), BF),
            pltpu.VMEM((K, tok, D), BF),
            pltpu.VMEM((2, chunks, nl - 1, K, T // nl, D), BF),
            pltpu.VMEM((tok, lat), BF),
            pltpu.VMEM((tok, lat), BF),
            pltpu.VMEM((2, chunks, nc - 1, T // nc, lat), BF),
            pltpu.VMEM((chunks, T // nc, lat), F32),
            pltpu.VMEM((8, lat), F32),
            pltpu.SemaphoreType.DMA((4,)),
            pltpu.SemaphoreType.DMA,
            pltpu.SemaphoreType.DMA((5, chunks, K, nl - 1)),
            pltpu.SemaphoreType.DMA((5, chunks, K, nl - 1)),
            pltpu.SemaphoreType.DMA((4, chunks, nc - 1)),
            pltpu.SemaphoreType.DMA((4, chunks, nc - 1)),
        ],
        compiler_params=pltpu.CompilerParams(
            collective_id=0, has_side_effects=True, vmem_limit_bytes=62 * 1024 * 1024
        ),
        cost_estimate=pl.CostEstimate(flops=flops, bytes_accessed=40 << 20, transcendentals=tok * ff),
    )(hidden_in, ln_gain, ln_bias, w_in, b_in, w_out, b_out, w_enc, b_enc[None, :], w_dec, b_dec)


def grads_kernel(acts, dres, feat, dpre, w_dec, genc, gbenc, gdec, flipped):
    K, tok, D = acts.shape
    scale = 1.0 / math.sqrt(tok)

    @pl.when(pl.program_id(0) == 0)
    def _():
        for k in range(K):
            flipped[k] = acts[k].T

    d = dpre[...]
    gbenc[...] = jnp.sum(d.astype(F32), 0, keepdims=True)
    for k in range(K):
        genc[k] = jnp.dot(flipped[k], d, preferred_element_type=F32).astype(BF)
    f = feat[...].T
    column = jnp.dot(f, jnp.ones((tok, 128), BF), preferred_element_type=F32)[:, 0:1]
    for k in range(K):
        w = w_dec[k].astype(F32)
        norms = jnp.sqrt(jnp.sum(w * w, -1, keepdims=True) + row_eps)
        main = jnp.dot(f, dres[k], preferred_element_type=F32)
        gdec[k] = (main + (sparsity_weight * scale * column / norms) * w).astype(BF)


def grads(acts, dres, feat, dpre, w_dec):
    K, tok, D = acts.shape
    lat = feat.shape[1]
    lt = min(256, lat)
    whole = pl.BlockSpec((K, tok, D), lambda i: (0, 0, 0))
    cols = pl.BlockSpec((tok, lt), lambda i: (0, i))
    deep = pl.BlockSpec((K, lt, D), lambda i: (0, i, 0))
    genc, gbenc, gdec = pl.pallas_call(
        grads_kernel,
        grid=(lat // lt,),
        out_shape=(
            jax.ShapeDtypeStruct((K, D, lat), BF),
            jax.ShapeDtypeStruct((1, lat), F32),
            jax.ShapeDtypeStruct((K, lat, D), BF),
        ),
        in_specs=[whole, whole, cols, cols, deep],
        out_specs=(
            pl.BlockSpec((K, D, lt), lambda i: (0, 0, i)),
            pl.BlockSpec((1, lt), lambda i: (0, i)),
            deep,
        ),
        scratch_shapes=[pltpu.VMEM((K, D, tok), BF)],
        compiler_params=pltpu.CompilerParams(vmem_limit_bytes=48 * 1024 * 1024),
    )(acts, dres, feat, dpre, w_dec)
    return genc, gbenc[0], gdec


def plain(hidden_in, ln_gain, ln_bias, w_in, b_in, w_out, b_out, w_enc, b_enc, w_dec, b_dec, total):
    tokens = hidden_in.shape[1]
    feat_cols = hidden_in.shape[2]
    scale = 1.0 / math.sqrt(tokens)
    lat_index = lax.axis_index("lat")
    whole = lax.all_gather(hidden_in, "lat", axis=2, tiled=True)
    floats = whole.astype(F32)
    center = floats - jnp.mean(floats, -1, keepdims=True)
    spread = jnp.mean(center * center, -1, keepdims=True)
    normed = (
        center * lax.rsqrt(spread + norm_eps) * ln_gain[:, None, :] + ln_bias[:, None, :]
    ).astype(BF)
    raised = jnp.einsum("ctd,cdf->ctf", normed, w_in, preferred_element_type=F32) + b_in[:, None, :]
    active = jax.nn.gelu(raised, approximate=False).astype(BF)
    terms = jnp.einsum("ctf,cfd->ctd", active, w_out, preferred_element_type=F32)
    share = lax.psum_scatter(terms, "lat", scatter_dimension=2, tiled=True)
    out_bias = lax.dynamic_slice_in_dim(b_out, lat_index * feat_cols, feat_cols, 1)
    piece = (hidden_in.astype(F32) + share + out_bias[:, None, :]).astype(BF)
    acts = lax.all_gather(piece, "lat", axis=2, tiled=True)
    pre_sum, total = lax.psum(
        (jnp.einsum("ctd,cdl->tl", acts, w_enc, preferred_element_type=F32), total), "ckpt"
    )
    pre = pre_sum + b_enc[None, :]
    feat = jnp.maximum(pre, 0.0).astype(BF)
    recon_terms = jnp.einsum("tl,cld->ctd", feat, w_dec, preferred_element_type=F32)
    recon = lax.psum(recon_terms.astype(BF), "lat").astype(F32)
    dres = ((recon + b_dec[:, None, :] - acts.astype(F32)) * scale).astype(BF)
    dfeat = lax.psum(
        jnp.einsum("ctd,cld->tl", dres, w_dec, preferred_element_type=F32).astype(BF), "ckpt"
    ).astype(F32) + (sparsity_weight * scale * total)[None, :]
    dpre = jnp.where(pre > 0.0, dfeat, 0.0).astype(BF)
    return acts, dres, feat, dpre


def on_device(nl, nc, hidden_in, ln_gain, ln_bias, w_in, b_in, w_out, b_out, w_enc, b_enc, w_dec, b_dec):
    K, tok, cols = hidden_in.shape
    scale = 1.0 / math.sqrt(tok)
    chunks = 2
    T = tok // chunks
    args = (hidden_in, ln_gain, ln_bias, w_in, b_in, w_out, b_out, w_enc, b_enc, w_dec, b_dec)
    if cols % 128 == 0 and T % (16 * nl) == 0 and T % (16 * nc) == 0:
        return grads(*fused(*args, nl, nc, chunks, 2), w_dec)
    wide_dec = w_dec.astype(F32)
    norms = jnp.sqrt(jnp.sum(wide_dec * wide_dec, 2) + row_eps)
    acts, dres, feat, dpre = plain(*args, jnp.sum(norms, 0))
    grad_enc = jnp.einsum("ctd,tl->cdl", acts, dpre, preferred_element_type=F32).astype(BF)
    grad_benc = jnp.sum(dpre.astype(F32), 0)
    column = jnp.sum(feat.astype(F32), 0)
    main = jnp.einsum("tl,ctd->cld", feat, dres, preferred_element_type=F32)
    extra = sparsity_weight * scale * column[None, :, None] * wide_dec / norms[:, :, None]
    grad_dec = (main + extra).astype(BF)
    return (grad_enc, grad_benc, grad_dec)


def solution(mesh):
    placed = (
        P("ckpt", None, "lat"),
        P("ckpt", None),
        P("ckpt", None),
        P("ckpt", None, "lat"),
        P("ckpt", "lat"),
        P("ckpt", "lat", None),
        P("ckpt", None),
        P("ckpt", None, "lat"),
        P("lat"),
        P("ckpt", "lat", None),
        P("ckpt", None),
    )
    return jax.shard_map(
        functools.partial(on_device, mesh.shape["lat"], mesh.shape["ckpt"]),
        mesh=mesh,
        in_specs=placed,
        out_specs=(P("ckpt", None, "lat"), P("lat"), P("ckpt", "lat", None)),
        check_vma=False,
    )
```
